512 devices in a mesh: dom: 32 (over z_lo, y), feat: 16 (over z_hi, x, core).
Axes of the slice: x: 4, y: 4, z: 16 (z_hi: 2, z_lo: 8; z = z_hi * 8 + z_lo), core: 2. Of those that a mesh axis runs over, the one named last changes fastest.
Arguments:
- features: bfloat16 [512, 256, 128], P('dom', 'feat'), may hold values from -6 to 6
- tiles: bfloat16 [32, 32, 4, 128, 128], P('dom'), may hold values from 0 to 0.26, as said below
- block_rows: int32 [32, 32, 4], P('dom'), may hold values from 0 to 15, as said below
- block_cols: int32 [32, 32, 4], P('dom'), may hold values from 0 to 15
- block_counts: int32 [32, 32], P('dom'), may hold values from 1 to 4, as said below
- weight_one: bfloat16 [256, 256], replicated, may hold values from -0.375 to 0.375
- bias_one: float32 [256], replicated, may hold values from -3 to 3
- weight_two: bfloat16 [256, 256], replicated, may hold values from -0.375 to 0.375
- bias_two: float32 [256], replicated, may hold values from -3 to 3
Outputs:
- node_out: float32 [512, 256, 128], P('dom', 'feat')
The draws below stay inside these ranges and needn't reach their ends.
Inputs may be any that keep to these rules, and one draw needn't show every extreme that they name: `tiles`: adjacency values are nonnegative. `block_rows`: within one pair of source and destination partitions the 4 slots name different row blocks. `block_counts`: slots at or past the count are not part of the operator. Each partition's pair with itself is full, and one destination partition is full from every source.
All inputs are finite; a program needn't handle non-finite values.
Results may differ from the reference program's by a relative error of at most 0.018.
Values may be sent and summed in bfloat16 or wider, within the bound.
No kernel may reach another device: no remote copies, remote signals or barrier semaphores. Data moves between devices by JAX's collectives and lax.ppermute only.
A program may use at most 64 MiB of HBM per device.

```python
import jax
import jax.numpy as jnp
from jax import lax

F = 256
H = 256
BLK = 128
NB_DEV = 16
CAP = 4
NBLK = 512
N_DOM = 32


def draw_tiles(key, part):
    key = jax.random.fold_in(key, 31)
    mask_key, value_key = jax.random.split(key, 2)
    shape = (N_DOM, N_DOM, CAP, BLK, BLK)
    linked = jax.random.randint(mask_key, shape, 0, BLK) < min(8, BLK // 2)
    values = jax.random.uniform(value_key, shape, jnp.float32, 0.02, 0.26)
    return jnp.where(linked, values, jnp.zeros_like(values)).astype(jnp.bfloat16)


def draw_block_rows(key, part):
    key = jax.random.fold_in(key, 11)
    keys = jax.random.split(key, N_DOM * N_DOM)
    chosen = jax.vmap(lambda one_key: jax.random.permutation(one_key, NB_DEV)[:CAP])(keys)
    return chosen.reshape(N_DOM, N_DOM, CAP).astype(jnp.int32)


def draw_block_counts(key, part):
    key = jax.random.fold_in(key, 23)
    starting_key, spike_key, popular_key = jax.random.split(key, 3)
    base_count = jax.random.randint(starting_key, (N_DOM, N_DOM), 1, 3)
    spike_draw = jax.random.randint(spike_key, (N_DOM, N_DOM), 0, 8) == 0
    popular_target = jax.random.randint(popular_key, (), 0, N_DOM)
    source_positions = lax.broadcasted_iota(jnp.int32, (N_DOM, N_DOM), 0)
    target_positions = lax.broadcasted_iota(jnp.int32, (N_DOM, N_DOM), 1)
    populated_slots = spike_draw | (source_positions == target_positions) | (target_positions == popular_target)
    return jnp.where(populated_slots, CAP, jnp.minimum(base_count, CAP)).astype(jnp.int32)


def touch_ends(values, own_key, smallest, largest):
    spot = [jax.random.randint(jax.random.fold_in(own_key, axis), (), 0, length) for axis, length in enumerate(values.shape)]
    main_axis = values.shape.index(max(values.shape))
    next_to = spot[:main_axis] + [(spot[main_axis] + 1) % values.shape[main_axis]] + spot[main_axis + 1:]
    return values.at[tuple(spot)].set(smallest).at[tuple(next_to)].set(largest)


def block_levels(rng, dims, cuts, low, largest):
    gain = 1.0
    for axis_at, parts in cuts:
        heights = jax.random.uniform(jax.random.fold_in(jax.random.fold_in(rng, 6), axis_at), (parts,), jnp.float32, low / len(cuts), largest / len(cuts))
        gain = gain * jnp.repeat(jnp.exp(heights), dims[axis_at] // parts).reshape((-1,) + (1,) * (len(dims) - 1 - axis_at))
    return gain


def scatter_about(rng, dims, scale, reach, cuts=(), held_as=jnp.bfloat16):
    array = jax.random.normal(rng, dims, jnp.float32) * scale
    if len(cuts) > 0:
        array = block_levels(rng, dims, cuts, -0.22, 0.18) * array
    return jnp.clip(array, min=-reach, max=reach).astype(held_as)


def setup_inputs(seed: int = 0) -> dict:
    streams_of = jax.random.split(jax.random.key(seed), 10)
    return {
        "features": scatter_about(streams_of[0], (NBLK, F, BLK), 1.0, 6.0, ((0, 32), (1, 16))),
        "tiles": draw_tiles(jax.random.fold_in(streams_of[9], 71), 0),
        "block_rows": draw_block_rows(jax.random.fold_in(streams_of[9], 71), 0),
        "block_cols": touch_ends(jax.random.randint(streams_of[3], (N_DOM, N_DOM, CAP), 0, NB_DEV), jax.random.fold_in(streams_of[3], 1), 0, NB_DEV - 1).astype(jnp.int32),
        "block_counts": draw_block_counts(jax.random.fold_in(streams_of[9], 71), 0),
        "weight_one": scatter_about(streams_of[5], (F, H), F ** -0.5, 0.375),
        "bias_one": scatter_about(streams_of[6], (H,), 0.5, 3.0, (), jnp.float32),
        "weight_two": scatter_about(streams_of[7], (H, H), H ** -0.5, 0.375),
        "bias_two": scatter_about(streams_of[8], (H,), 0.5, 3.0, (), jnp.float32),
    }


def aggregate(blocks, tiles, block_rows, block_cols, block_counts):
    width = blocks.shape[1]
    source = blocks.reshape(N_DOM, NB_DEV, width, BLK)
    src_index = jnp.arange(N_DOM, dtype=jnp.int32)[:, None]
    slot_index = jnp.arange(CAP, dtype=jnp.int32)[None, :]

    def one_target(target):
        tile_set = lax.dynamic_index_in_dim(tiles, target, 1, keepdims=False)
        row_index = lax.dynamic_index_in_dim(block_rows, target, 1, keepdims=False)
        col_index = lax.dynamic_index_in_dim(block_cols, target, 1, keepdims=False)
        counts_here = lax.dynamic_index_in_dim(block_counts, target, 1, keepdims=False)
        picked = source[src_index, col_index]
        terms = jnp.einsum("sjfk,sjik->sjfi", picked.astype(jnp.float32), tile_set.astype(jnp.float32))
        live_mask = slot_index < counts_here[:, None]
        terms = jnp.where(live_mask[:, :, None, None], terms, jnp.zeros_like(terms))
        rounded = lax.optimization_barrier(terms.astype(jnp.bfloat16)).astype(jnp.float32)
        totals = jnp.zeros((NB_DEV, width, BLK), jnp.float32)
        totals = totals.at[row_index.reshape(-1)].add(rounded.reshape(N_DOM * CAP, width, BLK))
        return totals.astype(jnp.bfloat16)

    targets = jnp.arange(N_DOM, dtype=jnp.int32)
    return lax.map(one_target, targets).reshape(N_DOM * NB_DEV, width, BLK)


def transform(blocks, weight, bias_vector):
    product = jnp.einsum("bfk,fh->bhk", blocks.astype(jnp.float32), weight.astype(jnp.float32))
    return product + bias_vector[None, :, None]


def reference(features, tiles, block_rows, block_cols, block_counts, weight_one, bias_one, weight_two, bias_two):
    agg_one = aggregate(features, tiles, block_rows, block_cols, block_counts)
    hidden = jax.nn.relu(transform(agg_one, weight_one, bias_one)).astype(jnp.bfloat16)
    agg_two = aggregate(hidden, tiles, block_rows, block_cols, block_counts)
    return transform(agg_two, weight_two, bias_two)
```

```python
import functools

import jax
import jax.numpy as jnp
from jax import lax
from jax.experimental import pallas as pl
from jax.experimental.pallas import tpu as pltpu
from jax.sharding import Mesh
from jax.sharding import PartitionSpec as P

QUADS, ZQ, YS, HS, XC = 2, 4, 4, 2, 8
CAP, BLK, FW, ROWS = 4, 128, 16, 16
MSG = CAP * FW
META = 8
BF, F32 = jnp.bfloat16, jnp.float32
VMEM = pl.BlockSpec(memory_space=pltpu.VMEM)
NT = (((1,), (1,)), ((), ()))
TN = (((0,), (0,)), ((), ()))


def terms_kernel(with_meta, q_ref, cols_ref, counts_ref, rows_ref, v_ref, tile_ref, out_ref):
    first = ((pl.program_id(0) ^ q_ref[0]) * ZQ + pl.program_id(1)) * YS
    for y in range(YS):
        p = first + y
        count = counts_ref[0, p]
        for j in range(CAP):
            block = v_ref[cols_ref[0, p, j]]
            term = lax.dot_general(block, tile_ref[0, y, j], NT, preferred_element_type=F32)
            term = jnp.where(j < count, term, 0.0).astype(BF)
            out_ref[0, y, 0, j * FW : (j + 1) * FW, :] = term
        if with_meta:
            lane = lax.broadcasted_iota(jnp.int32, (META, BLK), 1)
            slot = (lane // FW) % CAP
            place = lane % FW
            for j in range(CAP):
                place = jnp.where(slot == j, place + rows_ref[0, p, j] * FW, place)
            out_ref[0, y, 0, MSG:, :] = place.astype(F32).astype(BF)


def slot_terms(q, cols, counts, rows, values, tiles, with_meta):
    lines = MSG + META if with_meta else MSG
    msg = pl.pallas_call(
        functools.partial(terms_kernel, with_meta),
        grid_spec=pltpu.PrefetchScalarGridSpec(
            num_scalar_prefetch=4,
            grid=(QUADS, ZQ),
            in_specs=[
                pl.BlockSpec((ROWS, FW, BLK), lambda r, b, *_: (0, 0, 0)),
                pl.BlockSpec((1, YS, CAP, BLK, BLK), lambda r, b, q, *_: (0, (r ^ q[0]) * ZQ + b, 0, 0, 0)),
            ],
            out_specs=pl.BlockSpec((1, YS, 1, lines, BLK), lambda r, b, *_: (b, 0, r, 0, 0)),
        ),
        out_shape=jax.ShapeDtypeStruct((ZQ, YS, QUADS, lines, BLK), BF),
        compiler_params=pltpu.CompilerParams(vmem_limit_bytes=16 << 20),
        name="slot_terms",
    )(q, cols, counts, rows, values, tiles)
    return msg.reshape(ZQ * YS, QUADS * lines, BLK)


def placed_sum(msg_of, meta_of):
    total = jnp.zeros((ROWS * FW, BLK), F32)
    lane = lax.broadcasted_iota(jnp.int32, (META, BLK), 1)
    spot = lax.broadcasted_iota(jnp.int32, (ROWS * FW, BLK), 0).astype(F32)
    for s in range(0, ZQ * YS, 4):
        halves = []
        for t in (s, s + 2):
            place = jnp.where(lane < MSG, meta_of(t).astype(F32), meta_of(t + 1).astype(F32))
            place = jnp.concatenate([place] * (ROWS * FW // META), axis=0)
            halves.append(jnp.where(spot == place, 1.0, 0.0).astype(BF))
        put = jnp.concatenate(halves, axis=1)
        lines = jnp.concatenate([msg_of(s + i) for i in range(4)], axis=0)
        total += jnp.dot(put, lines, preferred_element_type=F32)
    return total


def first_sum_kernel(q_ref, msg_ref, out_ref):
    for r in range(QUADS):
        base = r * (MSG + META)
        total = placed_sum(
            lambda s: msg_ref[s, base : base + MSG, :],
            lambda s: msg_ref[s, base + MSG : base + MSG + META, :],
        ).astype(BF)
        for h in range(HS):
            out_ref[r ^ q_ref[0], h] = total


def second_sum_kernel(r, msg_ref, meta_ref, *refs):
    base = r * (MSG + META)
    total = placed_sum(
        lambda s: msg_ref[s, r * MSG : (r + 1) * MSG, :],
        lambda s: meta_ref[s, base + MSG : base + MSG + META, :],
    )
    if len(refs) == 2:
        bias_ref, out_ref = refs
        out_ref[...] = total + bias_ref[...]
    else:
        refs[0][...] = total.astype(BF)


def dense_kernel(agg_ref, w1_ref, b1_ref, w2_ref, out_ref):
    half = agg_ref.shape[0] // 2
    agg = agg_ref[:half].astype(F32) + agg_ref[half:].astype(F32)
    agg = jnp.concatenate([agg[:, i * FW : (i + 1) * FW, :].reshape(half * FW, BLK) for i in range(2)], axis=1)
    hidden = lax.dot_general(w1_ref[...], agg.astype(BF), TN, preferred_element_type=F32)
    hidden = jnp.maximum(hidden + b1_ref[...], 0.0).astype(BF)
    out = lax.dot_general(w2_ref[...], hidden, TN, preferred_element_type=F32).astype(BF)
    for i in range(2):
        out_ref[:, i] = out[:, i * BLK : (i + 1) * BLK].reshape(XC, FW, BLK)


def per_device(features, tiles, rows, cols, counts, w1, b1, w2, b2):
    q = lax.axis_index("q").astype(jnp.int32).reshape(1)
    h = lax.axis_index("h")
    w2_half = lax.dynamic_slice_in_dim(w2, h * (XC * FW), XC * FW, 1)
    b1_wide = jnp.broadcast_to(b1[:, None], (b1.shape[0], 2 * BLK))
    own = lax.axis_index(("h", "x", "c")) * FW
    b2_wide = jnp.broadcast_to(lax.dynamic_slice_in_dim(b2, own, FW)[None, :, None], (ROWS, FW, BLK))
    b2_wide = b2_wide.reshape(ROWS * FW, BLK)

    def quad_exchange(msg):
        return lax.all_to_all(msg, ("b", "y"), 0, 0, tiled=True)

    msg1 = quad_exchange(slot_terms(q, cols, counts, rows, features, tiles, True))
    sums = pl.pallas_call(
        first_sum_kernel,
        in_specs=[pl.BlockSpec(memory_space=pltpu.SMEM), VMEM],
        out_specs=VMEM,
        out_shape=jax.ShapeDtypeStruct((QUADS, HS, ROWS * FW, BLK), BF),
        name="first_sum",
    )(q, msg1)
    sums = sums.reshape(QUADS * HS * XC, 2 * FW, BLK)
    sums = lax.all_to_all(sums, ("q", "h", "x", "c"), 0, 0, tiled=True)
    z = pl.pallas_call(
        dense_kernel,
        in_specs=[VMEM] * 4,
        out_specs=VMEM,
        out_shape=jax.ShapeDtypeStruct((XC, 2, FW, BLK), BF),
        name="dense",
    )(sums, w1, b1_wide, w2_half)
    z = lax.all_to_all(z, ("x", "c"), 0, 0, tiled=True).reshape(ROWS, FW, BLK)

    msg2 = quad_exchange(slot_terms(q, cols, counts, rows, z, tiles, False))
    far = pl.pallas_call(
        functools.partial(second_sum_kernel, 1),
        in_specs=[VMEM] * 2,
        out_specs=VMEM,
        out_shape=jax.ShapeDtypeStruct((ROWS * FW, BLK), BF),
        name="far_sum",
    )(msg2, msg1)
    far = lax.ppermute(far, "q", [(0, 1), (1, 0)])
    near = pl.pallas_call(
        functools.partial(second_sum_kernel, 0),
        in_specs=[VMEM] * 3,
        out_specs=VMEM,
        out_shape=jax.ShapeDtypeStruct((ROWS * FW, BLK), F32),
        name="near_sum",
    )(msg2, msg1, b2_wide)
    return (near + far.astype(F32)).reshape(ROWS, FW, BLK)


def solution(mesh):
    fine = Mesh(mesh.devices.reshape(QUADS, ZQ, YS, HS, 4, 2), ("q", "b", "y", "h", "x", "c"))
    dom, feat = ("q", "b", "y"), ("h", "x", "c")
    placed = (
        P(dom, feat, None),
        P(dom, None, None, None, None),
        P(dom, None, None),
        P(dom, None, None),
        P(dom, None),
        P(),
        P(),
        P(),
        P(),
    )
    return jax.shard_map(
        per_device, mesh=fine, in_specs=placed, out_specs=P(dom, feat, None), check_vma=False
    )
```

```python
import functools

import jax
import jax.numpy as jnp
from jax import lax
from jax.experimental import pallas as pl
from jax.experimental.pallas import tpu as pltpu
from jax.sharding import Mesh
from jax.sharding import PartitionSpec as P

QUADS, ZQ, YS, HS, XC = 2, 4, 4, 2, 8
CAP, BLK, FW, ROWS = 4, 128, 16, 16
MSG = CAP * FW
META = 8
ROOM = pltpu.CompilerParams(vmem_limit_bytes=8 << 20)
BF, F32 = jnp.bfloat16, jnp.float32
VMEM = pl.BlockSpec(memory_space=pltpu.VMEM)
NT = (((1,), (1,)), ((), ()))
TN = (((0,), (0,)), ((), ()))


def terms_kernel(with_meta, *refs):
    tables, v_ref, tile_ref, out_ref = refs[: 2 + with_meta], *refs[2 + with_meta : 5 + with_meta]
    held, v_held, tile_held, sems = refs[5 + with_meta : -3], *refs[-3:]
    q = lax.axis_index("q").astype(jnp.int32)

    def first_of(step):
        return ((step // ZQ ^ q) * ZQ + step % ZQ) * YS

    small = list(zip((*tables, v_ref), (*held, v_held)))
    copies = [pltpu.make_async_copy(src, dst, sems.at[i]) for i, (src, dst) in enumerate(small)]
    for step in range(QUADS * ZQ):
        chunk = tile_ref.at[0, pl.ds(first_of(step), YS)]
        copies.append(pltpu.make_async_copy(chunk, tile_held.at[step], sems.at[len(copies)]))
    for copy in copies:
        copy.start()
    for copy in copies[: len(small)]:
        copy.wait()
    cols_ref, counts_ref = held[:2]
    for step in range(QUADS * ZQ):
        copies[len(small) + step].wait()
        for y in range(YS):
            p = first_of(step) + y
            count = counts_ref[0, p]
            at = (y, step % ZQ, step // ZQ)
            for j in range(0, CAP, 2):
                pair = jnp.concatenate([v_held[cols_ref[0, j + i, p]] for i in range(2)], axis=0)
                tiles = tile_held[step, y, j : j + 2].reshape(2 * BLK, BLK)
                term = lax.dot_general(pair, tiles, NT, preferred_element_type=F32)
                for i in range(2):
                    mine = term[i * FW : (i + 1) * FW, i * BLK : (i + 1) * BLK]
                    mine = jnp.where(j + i < count, mine, 0.0).astype(BF)
                    out_ref[*at, (j + i) * FW : (j + i + 1) * FW, :] = mine
            if with_meta:
                lane = lax.broadcasted_iota(jnp.int32, (META, BLK), 1)
                slot = (lane // FW) % CAP
                place = lane % FW
                for j in range(CAP):
                    place = jnp.where(slot == j, place + held[2][0, j, p] * FW, place)
                out_ref[*at, MSG:, :] = place.astype(F32).astype(BF)


def slot_terms(tables, values, tiles):
    with_meta = len(tables) == 3
    lines = MSG + META if with_meta else MSG
    steps = QUADS * ZQ
    hbm = pl.BlockSpec(memory_space=pltpu.HBM)
    msg = pl.pallas_call(
        functools.partial(terms_kernel, with_meta),
        in_specs=[hbm] * len(tables) + [pl.BlockSpec(memory_space=pl.ANY), hbm],
        out_specs=VMEM,
        out_shape=jax.ShapeDtypeStruct((YS, ZQ, QUADS, lines, BLK), BF),
        scratch_shapes=[pltpu.SMEM(table.shape, table.dtype) for table in tables]
        + [
            pltpu.VMEM(values.shape, values.dtype),
            pltpu.VMEM((steps, YS, CAP, BLK, BLK), BF),
            pltpu.SemaphoreType.DMA((len(tables) + 1 + steps,)),
        ],
        compiler_params=ROOM,
        name="slot_terms",
    )(*tables, values, tiles)
    return msg.reshape(YS * ZQ, QUADS * lines, BLK)


def in_hbm(array):
    return pltpu.with_memory_space_constraint(array, pltpu.HBM)


def placed_sum(msg_of, meta_of):
    total = jnp.zeros((ROWS * FW, BLK), F32)
    lane = lax.broadcasted_iota(jnp.int32, (META, BLK), 1)
    spot = lax.broadcasted_iota(jnp.int32, (ROWS * FW, BLK), 0).astype(F32)
    for s in range(0, ZQ * YS, 4):
        halves = []
        for t in (s, s + 2):
            place = jnp.where(lane < MSG, meta_of(t).astype(F32), meta_of(t + 1).astype(F32))
            place = jnp.concatenate([place] * (ROWS * FW // META), axis=0)
            halves.append(jnp.where(spot == place, 1.0, 0.0).astype(BF))
        put = jnp.concatenate(halves, axis=1)
        lines = jnp.concatenate([msg_of(s + i) for i in range(4)], axis=0)
        total += jnp.dot(put, lines, preferred_element_type=F32)
    return total


def first_sum_kernel(q_ref, msg_ref, out_ref):
    for r in range(QUADS):
        base = r * (MSG + META)
        total = placed_sum(
            lambda s: msg_ref[s, base : base + MSG, :],
            lambda s: msg_ref[s, base + MSG : base + MSG + META, :],
        ).astype(BF)
        for h in range(HS):
            out_ref[r ^ q_ref[0], h] = total


def second_sum_kernel(r, msg_ref, meta_ref, *refs):
    base = r * (MSG + META)
    total = placed_sum(
        lambda s: msg_ref[s, r * MSG : (r + 1) * MSG, :],
        lambda s: meta_ref[s, base + MSG : base + MSG + META, :],
    )
    if len(refs) == 2:
        bias_ref, out_ref = refs
        out_ref[...] = total + bias_ref[...]
    else:
        refs[0][...] = total.astype(BF)


def dense_kernel(agg_ref, w1_ref, b1_ref, w2_ref, out_ref):
    half = agg_ref.shape[0] // 2
    agg = agg_ref[:half].astype(F32) + agg_ref[half:].astype(F32)
    agg = jnp.concatenate([agg[:, i * FW : (i + 1) * FW, :].reshape(half * FW, BLK) for i in range(2)], axis=1)
    hidden = lax.dot_general(w1_ref[...], agg.astype(BF), TN, preferred_element_type=F32)
    bias = jnp.transpose(jnp.broadcast_to(b1_ref[...], (BLK, b1_ref.shape[1])))
    hidden = jnp.maximum(hidden + jnp.concatenate([bias, bias], axis=1), 0.0).astype(BF)
    out = lax.dot_general(w2_ref[...], hidden, TN, preferred_element_type=F32).astype(BF)
    for i in range(2):
        out_ref[:, i] = out[:, i * BLK : (i + 1) * BLK].reshape(XC, FW, BLK)


def per_device(features, tiles, rows, cols, counts, w1, b1, w2, b2):
    q = lax.axis_index("q").astype(jnp.int32).reshape(1)
    h = lax.axis_index("h")
    w2_half = lax.dynamic_slice_in_dim(w2, h * (XC * FW), XC * FW, 1)
    cols, rows = (jnp.swapaxes(table, 1, 2) for table in (cols, rows))
    cols, rows, counts, features, tiles = (in_hbm(array) for array in (cols, rows, counts, features, tiles))
    own = lax.axis_index(("h", "x", "c")) * FW
    b2_wide = jnp.broadcast_to(lax.dynamic_slice_in_dim(b2, own, FW)[None, :, None], (ROWS, FW, BLK))
    b2_wide = b2_wide.reshape(ROWS * FW, BLK)

    def quad_exchange(msg):
        return lax.all_to_all(msg, ("y", "b"), 0, 0, tiled=True)

    msg1 = quad_exchange(slot_terms((cols, counts, rows), features, tiles))
    sums = pl.pallas_call(
        first_sum_kernel,
        in_specs=[pl.BlockSpec(memory_space=pltpu.SMEM), VMEM],
        out_specs=VMEM,
        out_shape=jax.ShapeDtypeStruct((QUADS, HS, ROWS * FW, BLK), BF),
        compiler_params=ROOM,
        name="first_sum",
    )(q, msg1)
    sums = sums.reshape(QUADS * HS * XC, 2 * FW, BLK)
    sums = lax.all_to_all(sums, ("q", "h", "x", "c"), 0, 0, tiled=True)
    z = pl.pallas_call(
        dense_kernel,
        in_specs=[VMEM] * 4,
        out_specs=VMEM,
        out_shape=jax.ShapeDtypeStruct((XC, 2, FW, BLK), BF),
        compiler_params=ROOM,
        name="dense",
    )(sums, w1, b1[None, :], w2_half)
    z = lax.all_to_all(z, ("x", "c"), 0, 0, tiled=True).reshape(ROWS, FW, BLK)

    msg2 = quad_exchange(slot_terms((cols, counts), z, tiles))
    far = pl.pallas_call(
        functools.partial(second_sum_kernel, 1),
        in_specs=[VMEM] * 2,
        out_specs=VMEM,
        out_shape=jax.ShapeDtypeStruct((ROWS * FW, BLK), BF),
        compiler_params=ROOM,
        name="far_sum",
    )(msg2, msg1)
    far = lax.ppermute(far, "q", [(0, 1), (1, 0)])
    near = pl.pallas_call(
        functools.partial(second_sum_kernel, 0),
        in_specs=[VMEM] * 3,
        out_specs=VMEM,
        out_shape=jax.ShapeDtypeStruct((ROWS * FW, BLK), F32),
        compiler_params=ROOM,
        name="near_sum",
    )(msg2, msg1, b2_wide)
    return (near + far.astype(F32)).reshape(ROWS, FW, BLK)


def solution(mesh):
    fine = Mesh(mesh.devices.reshape(QUADS, ZQ, YS, HS, 4, 2), ("q", "b", "y", "h", "x", "c"))
    dom, feat = ("q", "b", "y"), ("h", "x", "c")
    placed = (
        P(dom, feat, None),
        P(dom, None, None, None, None),
        P(dom, None, None),
        P(dom, None, None),
        P(dom, None),
        P(),
        P(),
        P(),
        P(),
    )
    return jax.shard_map(
        per_device, mesh=fine, in_specs=placed, out_specs=P(dom, feat, None), check_vma=False
    )
```

```python
import functools

import jax
import jax.numpy as jnp
from jax import lax
from jax.experimental import pallas as pl
from jax.experimental.pallas import tpu as pltpu
from jax.sharding import Mesh
from jax.sharding import PartitionSpec as P

QUADS, ZQ, YS, HS, XS, CS = 2, 4, 4, 2, 4, 2
XC = XS * CS
STEPS = QUADS * ZQ
CAP, BLK, FW, ROWS = 4, 128, 16, 16
MSG = CAP * FW
BODY = QUADS * MSG
META = 8
LINES = ROWS * FW
BF, F32 = jnp.bfloat16, jnp.float32
VMEM = pl.BlockSpec(memory_space=pltpu.VMEM)
HBM = pl.BlockSpec(memory_space=pltpu.HBM)
NT = (((1,), (1,)), ((), ()))
TN = (((0,), (0,)), ((), ()))
ROOM = pltpu.CompilerParams(vmem_limit_bytes=8 << 20)


def in_hbm(array):
    return pltpu.with_memory_space_constraint(array, pltpu.HBM)


def target(step, y):
    q = lax.axis_index("q").astype(jnp.int32)
    return ((step // ZQ ^ q) * ZQ + step % ZQ) * YS + y


def write_terms(step, cols_ref, counts_ref, values_ref, tiles_ref, out_ref):
    for y in range(YS):
        p = target(step, y)
        count = counts_ref[0, p]
        for j in range(0, CAP, 2):
            pair = jnp.concatenate([values_ref[cols_ref[0, j + i, p]] for i in range(2)], axis=0)
            tiles = tiles_ref[step, y, j : j + 2].reshape(2 * BLK, BLK)
            term = lax.dot_general(pair, tiles, NT, preferred_element_type=F32)
            for i in range(2):
                mine = term[i * FW : (i + 1) * FW, i * BLK : (i + 1) * BLK]
                mine = jnp.where(j + i < count, mine, 0.0).astype(BF)
                at = (step // ZQ) * MSG + (j + i) * FW
                out_ref[y, step % ZQ, at : at + FW, :] = mine


def first_terms_kernel(
    cols_in, counts_in, rows_in, values_in, tiles_in, out_ref, tiles_ref, cols, counts, rows, values, sems
):
    small = list(zip((cols_in, counts_in, rows_in, values_in), (cols, counts, rows, values)))
    copies = [pltpu.make_async_copy(src, dst, sems.at[i]) for i, (src, dst) in enumerate(small)]
    for step in range(STEPS):
        chunk = tiles_in.at[0, pl.ds(target(step, 0), YS)]
        copies.append(pltpu.make_async_copy(chunk, tiles_ref.at[step], sems.at[len(copies)]))
    for copy in copies:
        copy.start()
    for copy in copies[: len(small)]:
        copy.wait()
    lane = lax.broadcasted_iota(jnp.int32, (META, BLK), 1)
    for b in range(ZQ):
        for y in range(YS):
            place = lane % FW
            for r in range(QUADS):
                for j in range(CAP):
                    row = rows[0, j, target(r * ZQ + b, y)]
                    place = jnp.where(lane // FW == r * CAP + j, place + row * FW, place)
            out_ref[y, b, BODY:, :] = place.astype(F32).astype(BF)
    for step in range(STEPS):
        copies[len(small) + step].wait()
        write_terms(step, cols, counts, values, tiles_ref, out_ref)


def second_terms_kernel(cols_in, counts_in, values_ref, tiles_ref, out_ref, cols, counts, sems):
    copies = [pltpu.make_async_copy(cols_in, cols, sems.at[0]), pltpu.make_async_copy(counts_in, counts, sems.at[1])]
    for copy in copies:
        copy.start()
    for copy in copies:
        copy.wait()
    for step in range(STEPS):
        write_terms(step, cols, counts, values_ref, tiles_ref, out_ref)


def placed_sum(r, msg_ref, meta_ref):
    total = jnp.zeros((LINES, BLK), F32)
    low = lax.broadcasted_iota(jnp.int32, (META, BLK), 1) < MSG
    spot = lax.broadcasted_iota(jnp.int32, (LINES, BLK), 0).astype(F32)
    for s in range(0, YS * ZQ, 4):
        halves = []
        for t in (s, s + 2):
            here, there = (meta_ref[t + i, BODY:, :].astype(F32) for i in range(2))
            if r == 0:
                there = pltpu.roll(there, MSG, 1)
            else:
                here = pltpu.roll(here, MSG, 1)
            place = jnp.concatenate([jnp.where(low, here, there)] * (LINES // META), axis=0)
            halves.append(jnp.where(spot == place, 1.0, 0.0).astype(BF))
        put = jnp.concatenate(halves, axis=1)
        lines = jnp.concatenate([msg_ref[s + i, r * MSG : (r + 1) * MSG, :] for i in range(4)], axis=0)
        total += jnp.dot(put, lines, preferred_element_type=F32)
    return total


def first_sum_kernel(msg_ref, out_ref):
    for r in range(QUADS):
        total = placed_sum(r, msg_ref, msg_ref).astype(BF)
        for h in range(HS):
            out_ref[r ^ lax.axis_index("q").astype(jnp.int32), h] = total


def far_sum_kernel(msg_ref, meta_ref, out_ref):
    out_ref[...] = placed_sum(1, msg_ref, meta_ref).astype(BF)


def column(bias_ref):
    return jnp.transpose(jnp.broadcast_to(bias_ref[...], (BLK, bias_ref.shape[1])))


def near_sum_kernel(msg_ref, meta_ref, bias_ref, out_ref, wide):
    wide[...] = column(bias_ref)
    h, x, c = (lax.axis_index(name).astype(jnp.int32) for name in ("h", "x", "c"))
    own = pl.multiple_of(((h * XS + x) * CS + c) * FW, FW)
    bias = jnp.concatenate([wide[pl.ds(own, FW), :]] * ROWS, axis=0)
    out_ref[...] = placed_sum(0, msg_ref, meta_ref) + bias


def dense_kernel(agg_ref, w1_ref, b1_ref, w2_ref, out_ref):
    half = agg_ref.shape[0] // 2
    agg = agg_ref[:half].astype(F32) + agg_ref[half:].astype(F32)
    agg = jnp.concatenate([agg[:, i * FW : (i + 1) * FW, :].reshape(half * FW, BLK) for i in range(2)], axis=1)
    hidden = lax.dot_general(w1_ref[...], agg.astype(BF), TN, preferred_element_type=F32)
    bias = column(b1_ref)
    hidden = jnp.maximum(hidden + jnp.concatenate([bias, bias], axis=1), 0.0).astype(BF)
    own = pl.multiple_of(lax.axis_index("h").astype(jnp.int32) * (XC * FW), XC * FW)
    out = lax.dot_general(w2_ref[:, pl.ds(own, XC * FW)], hidden, TN, preferred_element_type=F32).astype(BF)
    for i in range(2):
        out_ref[:, i] = out[:, i * BLK : (i + 1) * BLK].reshape(XC, FW, BLK)


def call(kernel, name, out_shape, *args, in_specs=None, scratch_shapes=()):
    return pl.pallas_call(
        kernel,
        in_specs=in_specs or [VMEM] * len(args),
        out_specs=jax.tree.map(lambda _: VMEM, out_shape),
        out_shape=out_shape,
        scratch_shapes=scratch_shapes,
        compiler_params=ROOM,
        name=name,
    )(*args)


def per_device(features, tiles, rows, cols, counts, w1, b1, w2, b2):
    cols, rows = (jnp.swapaxes(table, 1, 2) for table in (cols, rows))
    cols, rows, counts, features, tiles = (in_hbm(array) for array in (cols, rows, counts, features, tiles))
    b1, b2 = b1[None, :], b2[None, :]
    smem = [pltpu.SMEM(table.shape, table.dtype) for table in (cols, counts, rows)]
    copy_sems = pltpu.SemaphoreType.DMA

    def message(lines):
        return jax.ShapeDtypeStruct((YS, ZQ, lines, BLK), BF)

    def quad_exchange(msg):
        msg = msg.reshape(YS * ZQ, msg.shape[2], BLK)
        return lax.all_to_all(msg, ("y", "b"), 0, 0, tiled=True)

    msg1, held = call(
        first_terms_kernel,
        "first_terms",
        (message(BODY + META), pltpu.VMEM((STEPS, YS, CAP, BLK, BLK), BF)),
        cols,
        counts,
        rows,
        features,
        tiles,
        in_specs=[HBM] * 5,
        scratch_shapes=[*smem, pltpu.VMEM(features.shape, BF), copy_sems((4 + STEPS,))],
    )
    msg1 = quad_exchange(msg1)
    sums = call(first_sum_kernel, "first_sum", jax.ShapeDtypeStruct((QUADS, HS, LINES, BLK), BF), msg1)
    sums = sums.reshape(QUADS * HS * XC, 2 * FW, BLK)
    sums = lax.all_to_all(sums, ("q", "h", "x", "c"), 0, 0, tiled=True)
    z = call(dense_kernel, "dense", jax.ShapeDtypeStruct((XC, 2, FW, BLK), BF), sums, w1, b1, w2)
    z = lax.all_to_all(z, ("x", "c"), 0, 0, tiled=True).reshape(ROWS, FW, BLK)

    msg2 = call(
        second_terms_kernel,
        "second_terms",
        message(BODY),
        cols,
        counts,
        z,
        held,
        in_specs=[HBM, HBM, VMEM, VMEM],
        scratch_shapes=[*smem[:2], copy_sems((2,))],
    )
    msg2 = quad_exchange(msg2)
    far = call(far_sum_kernel, "far_sum", jax.ShapeDtypeStruct((LINES, BLK), BF), msg2, msg1)
    far = lax.ppermute(far, "q", [(0, 1), (1, 0)])
    near = call(
        near_sum_kernel,
        "near_sum",
        jax.ShapeDtypeStruct((LINES, BLK), F32),
        msg2,
        msg1,
        b2,
        scratch_shapes=[pltpu.VMEM((b2.shape[1], BLK), F32)],
    )
    return (near + far.astype(F32)).reshape(ROWS, FW, BLK)


def solution(mesh):
    fine = Mesh(mesh.devices.reshape(QUADS, ZQ, YS, HS, XS, CS), ("q", "b", "y", "h", "x", "c"))
    dom, feat = ("q", "b", "y"), ("h", "x", "c")
    placed = (
        P(dom, feat, None),
        P(dom, None, None, None, None),
        P(dom, None, None),
        P(dom, None, None),
        P(dom, None),
        P(),
        P(),
        P(),
        P(),
    )
    return jax.shard_map(
        per_device, mesh=fine, in_specs=placed, out_specs=P(dom, feat, None), check_vma=False
    )
```

```python
import functools

import jax
import jax.numpy as jnp
from jax import lax
from jax.experimental import pallas as pl
from jax.experimental.pallas import tpu as pltpu
from jax.sharding import Mesh
from jax.sharding import PartitionSpec as P

QUADS, ZQ, YS, HS, XS, CS = 2, 4, 4, 2, 4, 2
XC = XS * CS
STEPS = QUADS * ZQ
WAVE = 2
CAP, BLK, FW, ROWS = 4, 128, 16, 16
MSG = CAP * FW
BODY = QUADS * MSG
META = 8
LINES = ROWS * FW
BF, F32 = jnp.bfloat16, jnp.float32
VMEM = pl.BlockSpec(memory_space=pltpu.VMEM)
HBM = pl.BlockSpec(memory_space=pltpu.HBM)
NT = (((1,), (1,)), ((), ()))
TN = (((0,), (0,)), ((), ()))
ROOM = pltpu.CompilerParams(vmem_limit_bytes=8 << 20)


def in_hbm(array):
    return pltpu.with_memory_space_constraint(array, pltpu.HBM)


def target(step, y):
    q = lax.axis_index("q").astype(jnp.int32)
    return ((step // ZQ ^ q) * ZQ + step % ZQ) * YS + y


def write_terms(step, cols_ref, counts_ref, values_ref, tiles_ref, out_ref):
    for y in range(YS):
        p = target(step, y)
        count = counts_ref[0, p]
        for j in range(0, CAP, 2):
            pair = jnp.concatenate([values_ref[cols_ref[0, j + i, p]] for i in range(2)], axis=0)
            tiles = tiles_ref[step, y, j : j + 2].reshape(2 * BLK, BLK)
            term = lax.dot_general(pair, tiles, NT, preferred_element_type=F32)
            for i in range(2):
                mine = term[i * FW : (i + 1) * FW, i * BLK : (i + 1) * BLK]
                mine = jnp.where(j + i < count, mine, 0.0).astype(BF)
                at = (step // ZQ) * MSG + (j + i) * FW
                out_ref[step % ZQ, y, at : at + FW, :] = mine


def first_terms_kernel(
    cols_in, counts_in, rows_in, values_in, tiles_in, out_ref, tiles_ref, cols, counts, rows, values, sems
):
    small = list(zip((cols_in, counts_in, rows_in, values_in), (cols, counts, rows, values)))
    copies = [pltpu.make_async_copy(src, dst, sems.at[i]) for i, (src, dst) in enumerate(small)]
    for step in range(0, STEPS, WAVE):
        chunk = tiles_in.at[0, pl.ds(target(step, 0) // YS, WAVE)]
        copies.append(pltpu.make_async_copy(chunk, tiles_ref.at[pl.ds(step, WAVE)], sems.at[len(copies)]))
    for copy in copies:
        copy.start()
    for copy in copies[: len(small)]:
        copy.wait()
    lane = lax.broadcasted_iota(jnp.int32, (META, BLK), 1)
    for b in range(ZQ):
        for y in range(YS):
            place = lane % FW
            for r in range(QUADS):
                for j in range(CAP):
                    row = rows[0, j, target(r * ZQ + b, y)]
                    place = jnp.where(lane // FW == r * CAP + j, place + row * FW, place)
            out_ref[b, y, BODY:, :] = place.astype(F32).astype(BF)
    for step in range(STEPS):
        if step % WAVE == 0:
            copies[len(small) + step // WAVE].wait()
        write_terms(step, cols, counts, values, tiles_ref, out_ref)


def second_terms_kernel(cols_in, counts_in, values_ref, tiles_ref, out_ref, cols, counts, sems):
    copies = [pltpu.make_async_copy(cols_in, cols, sems.at[0]), pltpu.make_async_copy(counts_in, counts, sems.at[1])]
    for copy in copies:
        copy.start()
    for copy in copies:
        copy.wait()
    for step in range(STEPS):
        write_terms(step, cols, counts, values_ref, tiles_ref, out_ref)


def placed_sum(r, msg_ref, meta_ref):
    total = jnp.zeros((LINES, BLK), F32)
    low = lax.broadcasted_iota(jnp.int32, (META, BLK), 1) < MSG
    spot = lax.broadcasted_iota(jnp.int32, (LINES, BLK), 0).astype(F32)
    for s in range(0, ZQ * YS, 4):
        halves = []
        for t in (s, s + 2):
            here, there = (meta_ref[t + i, BODY:, :].astype(F32) for i in range(2))
            if r == 0:
                there = pltpu.roll(there, MSG, 1)
            else:
                here = pltpu.roll(here, MSG, 1)
            place = jnp.concatenate([jnp.where(low, here, there)] * (LINES // META), axis=0)
            halves.append(jnp.where(spot == place, 1.0, 0.0).astype(BF))
        put = jnp.concatenate(halves, axis=1)
        lines = jnp.concatenate([msg_ref[s + i, r * MSG : (r + 1) * MSG, :] for i in range(4)], axis=0)
        total += jnp.dot(put, lines, preferred_element_type=F32)
    return total


def first_sum_kernel(msg_ref, out_ref):
    for r in range(QUADS):
        total = placed_sum(r, msg_ref, msg_ref).astype(BF)
        for h in range(HS):
            out_ref[r ^ lax.axis_index("q").astype(jnp.int32), h] = total


def far_sum_kernel(msg_ref, meta_ref, out_ref):
    out_ref[...] = placed_sum(1, msg_ref, meta_ref).astype(BF)


def column(bias_ref):
    return jnp.transpose(jnp.broadcast_to(bias_ref[...], (BLK, bias_ref.shape[1])))


def near_sum_kernel(msg_ref, meta_ref, bias_ref, out_ref, wide):
    wide[...] = column(bias_ref)
    h, x, c = (lax.axis_index(name).astype(jnp.int32) for name in ("h", "x", "c"))
    own = pl.multiple_of(((h * XS + x) * CS + c) * FW, FW)
    bias = jnp.concatenate([wide[pl.ds(own, FW), :]] * ROWS, axis=0)
    out_ref[...] = placed_sum(0, msg_ref, meta_ref) + bias


def dense_kernel(agg_ref, w1_ref, b1_ref, w2_ref, out_ref):
    half = agg_ref.shape[0] // 2
    agg = agg_ref[:half].astype(F32) + agg_ref[half:].astype(F32)
    agg = jnp.concatenate([agg[:, i * FW : (i + 1) * FW, :].reshape(half * FW, BLK) for i in range(2)], axis=1)
    hidden = lax.dot_general(w1_ref[...], agg.astype(BF), TN, preferred_element_type=F32)
    bias = column(b1_ref)
    hidden = jnp.maximum(hidden + jnp.concatenate([bias, bias], axis=1), 0.0).astype(BF)
    own = pl.multiple_of(lax.axis_index("h").astype(jnp.int32) * (XC * FW), XC * FW)
    out = lax.dot_general(w2_ref[:, pl.ds(own, XC * FW)], hidden, TN, preferred_element_type=F32).astype(BF)
    for i in range(2):
        out_ref[:, i] = out[:, i * BLK : (i + 1) * BLK].reshape(XC, FW, BLK)


def call(kernel, name, out_shape, *args, in_specs=None, scratch_shapes=()):
    return pl.pallas_call(
        kernel,
        in_specs=in_specs or [VMEM] * len(args),
        out_specs=jax.tree.map(lambda _: VMEM, out_shape),
        out_shape=out_shape,
        scratch_shapes=scratch_shapes,
        compiler_params=ROOM,
        name=name,
    )(*args)


def per_device(features, tiles, rows, cols, counts, w1, b1, w2, b2):
    cols, rows = (jnp.swapaxes(table, 1, 2) for table in (cols, rows))
    cols, rows, counts, features = (in_hbm(array) for array in (cols, rows, counts, features))
    b1, b2 = b1[None, :], b2[None, :]
    smem = [pltpu.SMEM(table.shape, table.dtype) for table in (cols, counts, rows)]
    copy_sems = pltpu.SemaphoreType.DMA

    def message(lines):
        return jax.ShapeDtypeStruct((ZQ, YS, lines, BLK), BF)

    def quad_exchange(msg):
        msg = msg.reshape(ZQ * YS, msg.shape[2], BLK)
        return lax.all_to_all(msg, ("b", "y"), 0, 0, tiled=True)

    msg1, held = call(
        first_terms_kernel,
        "first_terms",
        (message(BODY + META), pltpu.VMEM((STEPS, YS, CAP, BLK, BLK), BF)),
        cols,
        counts,
        rows,
        features,
        in_hbm(tiles.reshape(1, STEPS, YS, CAP, BLK, BLK)),
        in_specs=[HBM] * 5,
        scratch_shapes=[*smem, pltpu.VMEM(features.shape, BF), copy_sems((4 + STEPS // WAVE,))],
    )
    msg1 = quad_exchange(msg1)
    sums = call(first_sum_kernel, "first_sum", jax.ShapeDtypeStruct((QUADS, HS, LINES, BLK), BF), msg1)
    sums = sums.reshape(QUADS * HS * XC, 2 * FW, BLK)
    sums = lax.all_to_all(sums, ("q", "h", "x", "c"), 0, 0, tiled=True)
    z = call(dense_kernel, "dense", jax.ShapeDtypeStruct((XC, 2, FW, BLK), BF), sums, w1, b1, w2)
    z = lax.all_to_all(z, ("x", "c"), 0, 0, tiled=True).reshape(ROWS, FW, BLK)

    msg2 = call(
        second_terms_kernel,
        "second_terms",
        message(BODY),
        cols,
        counts,
        z,
        held,
        in_specs=[HBM, HBM, VMEM, VMEM],
        scratch_shapes=[*smem[:2], copy_sems((2,))],
    )
    msg2 = quad_exchange(msg2)
    far = call(far_sum_kernel, "far_sum", jax.ShapeDtypeStruct((LINES, BLK), BF), msg2, msg1)
    far = lax.ppermute(far, "q", [(0, 1), (1, 0)])
    near = call(
        near_sum_kernel,
        "near_sum",
        jax.ShapeDtypeStruct((LINES, BLK), F32),
        msg2,
        msg1,
        b2,
        scratch_shapes=[pltpu.VMEM((b2.shape[1], BLK), F32)],
    )
    return (near + far.astype(F32)).reshape(ROWS, FW, BLK)


def solution(mesh):
    fine = Mesh(mesh.devices.reshape(QUADS, ZQ, YS, HS, XS, CS), ("q", "b", "y", "h", "x", "c"))
    dom, feat = ("q", "b", "y"), ("h", "x", "c")
    placed = (
        P(dom, feat, None),
        P(dom, None, None, None, None),
        P(dom, None, None),
        P(dom, None, None),
        P(dom, None),
        P(),
        P(),
        P(),
        P(),
    )
    return jax.shard_map(
        per_device, mesh=fine, in_specs=placed, out_specs=P(dom, feat, None), check_vma=False
    )
```

```python
import functools

import jax
import jax.numpy as jnp
from jax import lax
from jax.experimental import pallas as pl
from jax.experimental.pallas import tpu as pltpu
from jax.sharding import Mesh
from jax.sharding import PartitionSpec as P

QUADS, ZQ, YS, HS, XS, CS = 2, 4, 4, 2, 4, 2
XC = XS * CS
STEPS = QUADS * ZQ
WAVE = 2
CAP, BLK, FW, ROWS = 4, 128, 16, 16
MSG = CAP * FW
BODY = QUADS * MSG
META = 8
LINES = ROWS * FW
BF, F32 = jnp.bfloat16, jnp.float32


def led_by(first, size):
    order = [first] + [m for m in range(size) if m != first]
    return order, [order.index(m) for m in range(size)]


QUAD_ORDER, QUAD_PLACE = led_by(2 * YS + 2, ZQ * YS)
FEAT_FIRST = (0 * HS + 1) * XC + 2 * CS + 1
FEAT_ORDER, FEAT_PLACE = led_by(FEAT_FIRST, QUADS * HS * XC)
PLANE_ORDER, PLANE_PLACE = led_by(2 * CS + 1, XC)
VMEM = pl.BlockSpec(memory_space=pltpu.VMEM)
HBM = pl.BlockSpec(memory_space=pltpu.HBM)
NT = (((1,), (1,)), ((), ()))
TN = (((0,), (0,)), ((), ()))
ROOM = pltpu.CompilerParams(vmem_limit_bytes=8 << 20)


def in_hbm(array):
    return pltpu.with_memory_space_constraint(array, pltpu.HBM)


def target(step, y):
    q = lax.axis_index("q").astype(jnp.int32)
    return ((step // ZQ ^ q) * ZQ + step % ZQ) * YS + y


def write_terms(step, cols_ref, counts_ref, values_ref, tiles_ref, out_ref):
    for y in range(YS):
        p = target(step, y)
        count = counts_ref[0, p]
        for j in range(0, CAP, 2):
            pair = jnp.concatenate([values_ref[cols_ref[0, j + i, p]] for i in range(2)], axis=0)
            tiles = tiles_ref[step, y, j : j + 2].reshape(2 * BLK, BLK)
            term = lax.dot_general(pair, tiles, NT, preferred_element_type=F32)
            for i in range(2):
                mine = term[i * FW : (i + 1) * FW, i * BLK : (i + 1) * BLK]
                mine = jnp.where(j + i < count, mine, 0.0).astype(BF)
                at = (step // ZQ) * MSG + (j + i) * FW
                out_ref[QUAD_PLACE[step % ZQ * YS + y], at : at + FW, :] = mine


def first_terms_kernel(
    cols_in, counts_in, rows_in, values_in, tiles_in, out_ref, tiles_ref, cols, counts, rows, values, sems
):
    small = list(zip((cols_in, counts_in, rows_in, values_in), (cols, counts, rows, values)))
    copies = [pltpu.make_async_copy(src, dst, sems.at[i]) for i, (src, dst) in enumerate(small)]
    for step in range(0, STEPS, WAVE):
        chunk = tiles_in.at[0, pl.ds(target(step, 0) // YS, WAVE)]
        copies.append(pltpu.make_async_copy(chunk, tiles_ref.at[pl.ds(step, WAVE)], sems.at[len(copies)]))
    for copy in copies:
        copy.start()
    for copy in copies[: len(small)]:
        copy.wait()
    lane = lax.broadcasted_iota(jnp.int32, (META, BLK), 1)
    for b in range(ZQ):
        for y in range(YS):
            place = lane % FW
            for r in range(QUADS):
                for j in range(CAP):
                    row = rows[0, j, target(r * ZQ + b, y)]
                    place = jnp.where(lane // FW == r * CAP + j, place + row * FW, place)
            out_ref[QUAD_PLACE[b * YS + y], BODY:, :] = place.astype(F32).astype(BF)
    for step in range(STEPS):
        if step % WAVE == 0:
            copies[len(small) + step // WAVE].wait()
        write_terms(step, cols, counts, values, tiles_ref, out_ref)


def second_terms_kernel(cols_in, counts_in, values_ref, tiles_ref, out_ref, cols, counts, sems):
    copies = [pltpu.make_async_copy(cols_in, cols, sems.at[0]), pltpu.make_async_copy(counts_in, counts, sems.at[1])]
    for copy in copies:
        copy.start()
    for copy in copies:
        copy.wait()
    for step in range(STEPS):
        write_terms(step, cols, counts, values_ref, tiles_ref, out_ref)


def placed_sum(r, msg_ref, meta_ref):
    total = jnp.zeros((LINES, BLK), F32)
    low = lax.broadcasted_iota(jnp.int32, (META, BLK), 1) < MSG
    spot = lax.broadcasted_iota(jnp.int32, (LINES, BLK), 0).astype(F32)
    for s in range(0, ZQ * YS, 4):
        halves = []
        for t in (s, s + 2):
            here, there = (meta_ref[t + i, BODY:, :].astype(F32) for i in range(2))
            if r == 0:
                there = pltpu.roll(there, MSG, 1)
            else:
                here = pltpu.roll(here, MSG, 1)
            place = jnp.concatenate([jnp.where(low, here, there)] * (LINES // META), axis=0)
            halves.append(jnp.where(spot == place, 1.0, 0.0).astype(BF))
        put = jnp.concatenate(halves, axis=1)
        lines = jnp.concatenate([msg_ref[s + i, r * MSG : (r + 1) * MSG, :] for i in range(4)], axis=0)
        total += jnp.dot(put, lines, preferred_element_type=F32)
    return total


def first_sum_kernel(msg_ref, out_ref):
    for r in range(QUADS):
        total = placed_sum(r, msg_ref, msg_ref).astype(BF)
        quad = r ^ lax.axis_index("q").astype(jnp.int32)
        for h in range(HS):
            for e in range(XC):
                member = (quad * HS + h) * XC + e
                place = jnp.where(member == FEAT_FIRST, 0, member + (member < FEAT_FIRST).astype(jnp.int32))
                rows = PLANE_PLACE[e] * 2 * FW
                out_ref[place] = total[rows : rows + 2 * FW]


def far_sum_kernel(msg_ref, meta_ref, out_ref):
    out_ref[...] = placed_sum(1, msg_ref, meta_ref).astype(BF)


def column(bias_ref):
    return jnp.transpose(jnp.broadcast_to(bias_ref[...], (BLK, bias_ref.shape[1])))


def near_sum_kernel(msg_ref, meta_ref, bias_ref, out_ref, wide):
    wide[...] = column(bias_ref)
    h, x, c = (lax.axis_index(name).astype(jnp.int32) for name in ("h", "x", "c"))
    own = pl.multiple_of(((h * XS + x) * CS + c) * FW, FW)
    bias = jnp.concatenate([wide[pl.ds(own, FW), :]] * ROWS, axis=0)
    out_ref[...] = placed_sum(0, msg_ref, meta_ref) + bias


def dense_kernel(agg_ref, w1_ref, b1_ref, w2_ref, out_ref):
    half = HS * XC
    agg = [agg_ref[FEAT_PLACE[m]].astype(F32) + agg_ref[FEAT_PLACE[half + m]].astype(F32) for m in range(half)]
    agg = [jnp.concatenate([part[i * FW : (i + 1) * FW] for part in agg], axis=0) for i in range(2)]
    agg = jnp.concatenate(agg, axis=1)
    hidden = lax.dot_general(w1_ref[...], agg.astype(BF), TN, preferred_element_type=F32)
    bias = column(b1_ref)
    hidden = jnp.maximum(hidden + jnp.concatenate([bias, bias], axis=1), 0.0).astype(BF)
    own = pl.multiple_of(lax.axis_index("h").astype(jnp.int32) * (XC * FW), XC * FW)
    out = lax.dot_general(w2_ref[:, pl.ds(own, XC * FW)], hidden, TN, preferred_element_type=F32).astype(BF)
    for i in range(2):
        for e in range(XC):
            out_ref[PLANE_PLACE[e], i] = out[e * FW : (e + 1) * FW, i * BLK : (i + 1) * BLK]


def call(kernel, name, out_shape, *args, in_specs=None, scratch_shapes=()):
    return pl.pallas_call(
        kernel,
        in_specs=in_specs or [VMEM] * len(args),
        out_specs=jax.tree.map(lambda _: VMEM, out_shape),
        out_shape=out_shape,
        scratch_shapes=scratch_shapes,
        compiler_params=ROOM,
        name=name,
    )(*args)


def per_device(features, tiles, rows, cols, counts, w1, b1, w2, b2):
    cols, rows = (jnp.swapaxes(table, 1, 2) for table in (cols, rows))
    cols, rows, counts, features = (in_hbm(array) for array in (cols, rows, counts, features))
    b1, b2 = b1[None, :], b2[None, :]
    smem = [pltpu.SMEM(table.shape, table.dtype) for table in (cols, counts, rows)]
    copy_sems = pltpu.SemaphoreType.DMA

    def message(lines):
        return jax.ShapeDtypeStruct((ZQ * YS, lines, BLK), BF)

    def quad_exchange(msg):
        return lax.all_to_all(msg, ("b", "y"), 0, 0, axis_index_groups=[QUAD_ORDER], tiled=True)

    msg1, held = call(
        first_terms_kernel,
        "first_terms",
        (message(BODY + META), pltpu.VMEM((STEPS, YS, CAP, BLK, BLK), BF)),
        cols,
        counts,
        rows,
        features,
        in_hbm(tiles.reshape(1, STEPS, YS, CAP, BLK, BLK)),
        in_specs=[HBM] * 5,
        scratch_shapes=[*smem, pltpu.VMEM(features.shape, BF), copy_sems((4 + STEPS // WAVE,))],
    )
    msg1 = quad_exchange(msg1)
    sums = call(first_sum_kernel, "first_sum", jax.ShapeDtypeStruct((QUADS * HS * XC, 2 * FW, BLK), BF), msg1)
    sums = lax.all_to_all(sums, ("q", "h", "x", "c"), 0, 0, axis_index_groups=[FEAT_ORDER], tiled=True)
    z = call(dense_kernel, "dense", jax.ShapeDtypeStruct((XC, 2, FW, BLK), BF), sums, w1, b1, w2)
    z = lax.all_to_all(z, ("x", "c"), 0, 0, axis_index_groups=[PLANE_ORDER], tiled=True).reshape(ROWS, FW, BLK)

    msg2 = call(
        second_terms_kernel,
        "second_terms",
        message(BODY),
        cols,
        counts,
        z,
        held,
        in_specs=[HBM, HBM, VMEM, VMEM],
        scratch_shapes=[*smem[:2], copy_sems((2,))],
    )
    msg2 = quad_exchange(msg2)
    far = call(far_sum_kernel, "far_sum", jax.ShapeDtypeStruct((LINES, BLK), BF), msg2, msg1)
    far = lax.ppermute(far, "q", [(0, 1), (1, 0)])
    near = call(
        near_sum_kernel,
        "near_sum",
        jax.ShapeDtypeStruct((LINES, BLK), F32),
        msg2,
        msg1,
        b2,
        scratch_shapes=[pltpu.VMEM((b2.shape[1], BLK), F32)],
    )
    return (near + far.astype(F32)).reshape(ROWS, FW, BLK)


def solution(mesh):
    fine = Mesh(mesh.devices.reshape(QUADS, ZQ, YS, HS, XS, CS), ("q", "b", "y", "h", "x", "c"))
    dom, feat = ("q", "b", "y"), ("h", "x", "c")
    placed = (
        P(dom, feat, None),
        P(dom, None, None, None, None),
        P(dom, None, None),
        P(dom, None, None),
        P(dom, None),
        P(),
        P(),
        P(),
        P(),
    )
    return jax.shard_map(
        per_device, mesh=fine, in_specs=placed, out_specs=P(dom, feat, None), check_vma=False
    )
```

```python
import functools

import jax
import jax.numpy as jnp
from jax import lax
from jax.experimental import pallas as pl
from jax.experimental.pallas import tpu as pltpu
from jax.sharding import Mesh
from jax.sharding import PartitionSpec as P

QUADS, ZQ, YS, HS, XS, CS = 2, 4, 4, 2, 4, 2
XC = XS * CS
STEPS = QUADS * ZQ
WAVE = 2
CAP, BLK, FW, ROWS = 4, 128, 16, 16
MSG = CAP * FW
BODY = QUADS * MSG
META = 8
LINES = ROWS * FW
BF, F32 = jnp.bfloat16, jnp.float32


def led_by(first, size):
    order = [first] + [m for m in range(size) if m != first]
    return order, [order.index(m) for m in range(size)]


QUAD_ORDER, QUAD_PLACE = led_by(1 * YS + 2, ZQ * YS)
FEAT_FIRST = (0 * HS + 1) * XC + 2 * CS + 1
FEAT_ORDER, FEAT_PLACE = led_by(FEAT_FIRST, QUADS * HS * XC)
PLANE_ORDER, PLANE_PLACE = led_by(2 * CS + 1, XC)
VMEM = pl.BlockSpec(memory_space=pltpu.VMEM)
HBM = pl.BlockSpec(memory_space=pltpu.HBM)
NT = (((1,), (1,)), ((), ()))
TN = (((0,), (0,)), ((), ()))
ROOM = pltpu.CompilerParams(vmem_limit_bytes=8 << 20)


def in_hbm(array):
    return pltpu.with_memory_space_constraint(array, pltpu.HBM)


def target(step, y):
    q = lax.axis_index("q").astype(jnp.int32)
    return ((step // ZQ ^ q) * ZQ + step % ZQ) * YS + y


def write_terms(step, cols_ref, counts_ref, values_ref, tiles_ref, out_ref):
    for y in range(YS):
        p = target(step, y)
        count = counts_ref[0, p]
        for j in range(0, CAP, 2):
            pair = jnp.concatenate([values_ref[cols_ref[0, j + i, p]] for i in range(2)], axis=0)
            tiles = tiles_ref[step, y, j : j + 2].reshape(2 * BLK, BLK)
            term = lax.dot_general(pair, tiles, NT, preferred_element_type=F32)
            for i in range(2):
                mine = term[i * FW : (i + 1) * FW, i * BLK : (i + 1) * BLK]
                mine = jnp.where(j + i < count, mine, 0.0).astype(BF)
                at = (step // ZQ) * MSG + (j + i) * FW
                out_ref[QUAD_PLACE[step % ZQ * YS + y], at : at + FW, :] = mine


def first_terms_kernel(
    cols_in, counts_in, rows_in, values_in, tiles_in, out_ref, tiles_ref, cols, counts, rows, values, sems
):
    small = list(zip((cols_in, counts_in, rows_in, values_in), (cols, counts, rows, values)))
    copies = [pltpu.make_async_copy(src, dst, sems.at[i]) for i, (src, dst) in enumerate(small)]
    for step in range(0, STEPS, WAVE):
        chunk = tiles_in.at[0, pl.ds(target(step, 0) // YS, WAVE)]
        copies.append(pltpu.make_async_copy(chunk, tiles_ref.at[pl.ds(step, WAVE)], sems.at[len(copies)]))
    for copy in copies:
        copy.start()
    for copy in copies[: len(small)]:
        copy.wait()
    lane = lax.broadcasted_iota(jnp.int32, (META, BLK), 1)
    for b in range(ZQ):
        for y in range(YS):
            place = lane % FW
            for r in range(QUADS):
                for j in range(CAP):
                    row = rows[0, j, target(r * ZQ + b, y)]
                    place = jnp.where(lane // FW == r * CAP + j, place + row * FW, place)
            out_ref[QUAD_PLACE[b * YS + y], BODY:, :] = place.astype(F32).astype(BF)
    for step in range(STEPS):
        if step % WAVE == 0:
            copies[len(small) + step // WAVE].wait()
        write_terms(step, cols, counts, values, tiles_ref, out_ref)


def second_terms_kernel(cols_in, counts_in, values_ref, tiles_ref, out_ref, cols, counts, sems):
    copies = [pltpu.make_async_copy(cols_in, cols, sems.at[0]), pltpu.make_async_copy(counts_in, counts, sems.at[1])]
    for copy in copies:
        copy.start()
    for copy in copies:
        copy.wait()
    for step in range(STEPS):
        write_terms(step, cols, counts, values_ref, tiles_ref, out_ref)


def placed_sum(r, msg_ref, meta_ref):
    total = jnp.zeros((LINES, BLK), F32)
    low = lax.broadcasted_iota(jnp.int32, (META, BLK), 1) < MSG
    spot = lax.broadcasted_iota(jnp.int32, (LINES, BLK), 0).astype(F32)
    for s in range(0, ZQ * YS, 4):
        halves = []
        for t in (s, s + 2):
            here, there = (meta_ref[t + i, BODY:, :].astype(F32) for i in range(2))
            if r == 0:
                there = pltpu.roll(there, MSG, 1)
            else:
                here = pltpu.roll(here, MSG, 1)
            place = jnp.concatenate([jnp.where(low, here, there)] * (LINES // META), axis=0)
            halves.append(jnp.where(spot == place, 1.0, 0.0).astype(BF))
        put = jnp.concatenate(halves, axis=1)
        lines = jnp.concatenate([msg_ref[s + i, r * MSG : (r + 1) * MSG, :] for i in range(4)], axis=0)
        total += jnp.dot(put, lines, preferred_element_type=F32)
    return total


def first_sum_kernel(msg_ref, out_ref):
    for r in range(QUADS):
        total = placed_sum(r, msg_ref, msg_ref).astype(BF)
        quad = r ^ lax.axis_index("q").astype(jnp.int32)
        for h in range(HS):
            for e in range(XC):
                member = (quad * HS + h) * XC + e
                place = jnp.where(member == FEAT_FIRST, 0, member + (member < FEAT_FIRST).astype(jnp.int32))
                rows = PLANE_PLACE[e] * 2 * FW
                out_ref[place] = total[rows : rows + 2 * FW]


def far_sum_kernel(msg_ref, meta_ref, out_ref):
    out_ref[...] = placed_sum(1, msg_ref, meta_ref).astype(BF)


def column(bias_ref):
    return jnp.transpose(jnp.broadcast_to(bias_ref[...], (BLK, bias_ref.shape[1])))


def near_sum_kernel(msg_ref, meta_ref, bias_ref, out_ref, wide):
    wide[...] = column(bias_ref)
    h, x, c = (lax.axis_index(name).astype(jnp.int32) for name in ("h", "x", "c"))
    own = pl.multiple_of(((h * XS + x) * CS + c) * FW, FW)
    bias = jnp.concatenate([wide[pl.ds(own, FW), :]] * ROWS, axis=0)
    out_ref[...] = placed_sum(0, msg_ref, meta_ref) + bias


def dense_kernel(agg_ref, w1_ref, b1_ref, w2_ref, out_ref):
    half = HS * XC
    agg = [agg_ref[FEAT_PLACE[m]].astype(F32) + agg_ref[FEAT_PLACE[half + m]].astype(F32) for m in range(half)]
    agg = [jnp.concatenate([part[i * FW : (i + 1) * FW] for part in agg], axis=0) for i in range(2)]
    agg = jnp.concatenate(agg, axis=1)
    hidden = lax.dot_general(w1_ref[...], agg.astype(BF), TN, preferred_element_type=F32)
    bias = column(b1_ref)
    hidden = jnp.maximum(hidden + jnp.concatenate([bias, bias], axis=1), 0.0).astype(BF)
    own = pl.multiple_of(lax.axis_index("h").astype(jnp.int32) * (XC * FW), XC * FW)
    out = lax.dot_general(w2_ref[:, pl.ds(own, XC * FW)], hidden, TN, preferred_element_type=F32).astype(BF)
    for i in range(2):
        for e in range(XC):
            out_ref[PLANE_PLACE[e], i] = out[e * FW : (e + 1) * FW, i * BLK : (i + 1) * BLK]


def call(kernel, name, out_shape, *args, in_specs=None, scratch_shapes=()):
    return pl.pallas_call(
        kernel,
        in_specs=in_specs or [VMEM] * len(args),
        out_specs=jax.tree.map(lambda _: VMEM, out_shape),
        out_shape=out_shape,
        scratch_shapes=scratch_shapes,
        compiler_params=ROOM,
        name=name,
    )(*args)


def per_device(features, tiles, rows, cols, counts, w1, b1, w2, b2):
    cols, rows = (jnp.swapaxes(table, 1, 2) for table in (cols, rows))
    cols, rows, counts, features = (in_hbm(array) for array in (cols, rows, counts, features))
    b1, b2 = b1[None, :], b2[None, :]
    smem = [pltpu.SMEM(table.shape, table.dtype) for table in (cols, counts, rows)]
    copy_sems = pltpu.SemaphoreType.DMA

    def message(lines):
        return jax.ShapeDtypeStruct((ZQ * YS, lines, BLK), BF)

    def quad_exchange(msg):
        return lax.all_to_all(msg, ("b", "y"), 0, 0, axis_index_groups=[QUAD_ORDER], tiled=True)

    msg1, held = call(
        first_terms_kernel,
        "first_terms",
        (message(BODY + META), pltpu.VMEM((STEPS, YS, CAP, BLK, BLK), BF)),
        cols,
        counts,
        rows,
        features,
        in_hbm(tiles.reshape(1, STEPS, YS, CAP, BLK, BLK)),
        in_specs=[HBM] * 5,
        scratch_shapes=[*smem, pltpu.VMEM(features.shape, BF), copy_sems((4 + STEPS // WAVE,))],
    )
    msg1 = quad_exchange(msg1)
    sums = call(first_sum_kernel, "first_sum", jax.ShapeDtypeStruct((QUADS * HS * XC, 2 * FW, BLK), BF), msg1)
    sums = lax.all_to_all(sums, ("q", "h", "x", "c"), 0, 0, axis_index_groups=[FEAT_ORDER], tiled=True)
    z = call(dense_kernel, "dense", jax.ShapeDtypeStruct((XC, 2, FW, BLK), BF), sums, w1, b1, w2)
    z = lax.all_to_all(z, ("x", "c"), 0, 0, axis_index_groups=[PLANE_ORDER], tiled=True).reshape(ROWS, FW, BLK)

    msg2 = call(
        second_terms_kernel,
        "second_terms",
        message(BODY),
        cols,
        counts,
        z,
        held,
        in_specs=[HBM, HBM, VMEM, VMEM],
        scratch_shapes=[*smem[:2], copy_sems((2,))],
    )
    msg2 = quad_exchange(msg2)
    far = call(far_sum_kernel, "far_sum", jax.ShapeDtypeStruct((LINES, BLK), BF), msg2, msg1)
    far = lax.ppermute(far, "q", [(0, 1), (1, 0)])
    near = call(
        near_sum_kernel,
        "near_sum",
        jax.ShapeDtypeStruct((LINES, BLK), F32),
        msg2,
        msg1,
        b2,
        scratch_shapes=[pltpu.VMEM((b2.shape[1], BLK), F32)],
    )
    return (near + far.astype(F32)).reshape(ROWS, FW, BLK)


def solution(mesh):
    fine = Mesh(mesh.devices.reshape(QUADS, ZQ, YS, HS, XS, CS), ("q", "b", "y", "h", "x", "c"))
    dom, feat = ("q", "b", "y"), ("h", "x", "c")
    placed = (
        P(dom, feat, None),
        P(dom, None, None, None, None),
        P(dom, None, None),
        P(dom, None, None),
        P(dom, None),
        P(),
        P(),
        P(),
        P(),
    )
    return jax.shard_map(
        per_device, mesh=fine, in_specs=placed, out_specs=P(dom, feat, None), check_vma=False
    )
```

```python
import functools

import jax
import jax.numpy as jnp
from jax import lax
from jax.experimental import pallas as pl
from jax.experimental.pallas import tpu as pltpu
from jax.sharding import Mesh
from jax.sharding import PartitionSpec as P

QUADS, ZQ, YS, HS, XS, CS = 2, 4, 4, 2, 4, 2
XC = XS * CS
STEPS = QUADS * ZQ
WAVE = 2
CAP, BLK, FW, ROWS = 4, 128, 16, 16
MSG = CAP * FW
BODY = QUADS * MSG
META = 8
LINES = ROWS * FW
BF, F32 = jnp.bfloat16, jnp.float32


def led_by(first, size):
    order = [first] + [m for m in range(size) if m != first]
    return order, [order.index(m) for m in range(size)]


QUAD_ORDER, QUAD_PLACE = led_by(1 * YS + 2, ZQ * YS)
FEAT_FIRST = (0 * HS + 1) * XC + 2 * CS + 1
FEAT_ORDER, FEAT_PLACE = led_by(FEAT_FIRST, QUADS * HS * XC)
PLANE_ORDER, PLANE_PLACE = led_by(2 * CS + 1, XC)
VMEM = pl.BlockSpec(memory_space=pltpu.VMEM)
HBM = pl.BlockSpec(memory_space=pltpu.HBM)
NT = (((1,), (1,)), ((), ()))
TN = (((0,), (0,)), ((), ()))
ROOM = pltpu.CompilerParams(vmem_limit_bytes=8 << 20)


def in_hbm(array):
    return pltpu.with_memory_space_constraint(array, pltpu.HBM)


def target(step, y):
    q = lax.axis_index("q").astype(jnp.int32)
    return ((step // ZQ ^ q) * ZQ + step % ZQ) * YS + y


def write_terms(step, cols_ref, counts_ref, values_ref, tiles_ref, out_ref):
    for y in range(YS):
        p = target(step, y)
        count = counts_ref[0, p]
        for j in range(0, CAP, 2):
            pair = jnp.concatenate([values_ref[cols_ref[0, j + i, p]] for i in range(2)], axis=0)
            tiles = tiles_ref[step, y, j : j + 2].reshape(2 * BLK, BLK)
            term = lax.dot_general(pair, tiles, NT, preferred_element_type=F32)
            for i in range(2):
                mine = term[i * FW : (i + 1) * FW, i * BLK : (i + 1) * BLK]
                mine = jnp.where(j + i < count, mine, 0.0).astype(BF)
                at = (step // ZQ) * MSG + (j + i) * FW
                out_ref[QUAD_PLACE[step % ZQ * YS + y], at : at + FW, :] = mine


def first_terms_kernel(
    cols_in, counts_in, rows_in, values_in, tiles_in, out_ref, tiles_ref, pick_ref, cols, counts, rows, values, sems
):
    small = list(zip((cols_in, counts_in, rows_in, values_in), (cols, counts, rows, values)))
    copies = [pltpu.make_async_copy(src, dst, sems.at[i]) for i, (src, dst) in enumerate(small)]
    for step in range(0, STEPS, WAVE):
        chunk = tiles_in.at[0, pl.ds(target(step, 0) // YS, WAVE)]
        copies.append(pltpu.make_async_copy(chunk, tiles_ref.at[pl.ds(step, WAVE)], sems.at[len(copies)]))
    for copy in copies:
        copy.start()
    for copy in copies[: len(small)]:
        copy.wait()
    lane = lax.broadcasted_iota(jnp.int32, (META, BLK), 1)
    for b in range(ZQ):
        for y in range(YS):
            place = lane % FW
            for r in range(QUADS):
                for j in range(CAP):
                    row = rows[0, j, target(r * ZQ + b, y)]
                    place = jnp.where(lane // FW == r * CAP + j, place + row * FW, place)
            out_ref[QUAD_PLACE[b * YS + y], BODY:, :] = place.astype(F32).astype(BF)
    shape = (FW, LINES)
    gap = lax.broadcasted_iota(jnp.int32, shape, 1) - lax.broadcasted_iota(jnp.int32, shape, 0)
    for step in range(STEPS):
        for y in range(YS):
            p = target(step, y)
            for j in range(CAP):
                start = jnp.where(j < counts[0, p], cols[0, j, p] * FW, -LINES)
                at = ((step * YS + y) * CAP + j) * FW
                pick_ref[at : at + FW, :] = jnp.where(gap == start, 1.0, 0.0).astype(BF)
    for step in range(STEPS):
        if step % WAVE == 0:
            copies[len(small) + step // WAVE].wait()
        write_terms(step, cols, counts, values, tiles_ref, out_ref)


def second_terms_kernel(pick_ref, values_ref, tiles_ref, out_ref):
    values = values_ref[...].reshape(LINES, BLK)
    lines = YS * MSG
    for step in range(STEPS):
        pick = pick_ref[step * lines : (step + 1) * lines, :]
        picked = jnp.dot(pick, values, preferred_element_type=F32).astype(BF)
        for y in range(YS):
            for j in range(0, CAP, 2):
                at = y * MSG + j * FW
                tiles = tiles_ref[step, y, j : j + 2].reshape(2 * BLK, BLK)
                term = lax.dot_general(picked[at : at + 2 * FW], tiles, NT, preferred_element_type=F32).astype(BF)
                for i in range(2):
                    mine = term[i * FW : (i + 1) * FW, i * BLK : (i + 1) * BLK]
                    to = (step // ZQ) * MSG + (j + i) * FW
                    out_ref[QUAD_PLACE[step % ZQ * YS + y], to : to + FW, :] = mine


def placed_sum(r, msg_ref, meta_ref):
    total = jnp.zeros((LINES, BLK), F32)
    low = lax.broadcasted_iota(jnp.int32, (META, BLK), 1) < MSG
    spot = lax.broadcasted_iota(jnp.int32, (LINES, BLK), 0).astype(F32)
    for s in range(0, ZQ * YS, 4):
        halves = []
        for t in (s, s + 2):
            here, there = (meta_ref[t + i, BODY:, :].astype(F32) for i in range(2))
            if r == 0:
                there = pltpu.roll(there, MSG, 1)
            else:
                here = pltpu.roll(here, MSG, 1)
            place = jnp.concatenate([jnp.where(low, here, there)] * (LINES // META), axis=0)
            halves.append(jnp.where(spot == place, 1.0, 0.0).astype(BF))
        put = jnp.concatenate(halves, axis=1)
        lines = jnp.concatenate([msg_ref[s + i, r * MSG : (r + 1) * MSG, :] for i in range(4)], axis=0)
        total += jnp.dot(put, lines, preferred_element_type=F32)
    return total


def first_sum_kernel(msg_ref, out_ref):
    for r in range(QUADS):
        total = placed_sum(r, msg_ref, msg_ref).astype(BF)
        quad = r ^ lax.axis_index("q").astype(jnp.int32)
        for h in range(HS):
            for e in range(XC):
                member = (quad * HS + h) * XC + e
                place = jnp.where(member == FEAT_FIRST, 0, member + (member < FEAT_FIRST).astype(jnp.int32))
                rows = PLANE_PLACE[e] * 2 * FW
                out_ref[place] = total[rows : rows + 2 * FW]


def far_sum_kernel(msg_ref, meta_ref, out_ref):
    out_ref[...] = placed_sum(1, msg_ref, meta_ref).astype(BF)


def column(bias_ref):
    return jnp.transpose(jnp.broadcast_to(bias_ref[...], (BLK, bias_ref.shape[1])))


def near_sum_kernel(msg_ref, meta_ref, bias_ref, out_ref, wide):
    wide[...] = column(bias_ref)
    h, x, c = (lax.axis_index(name).astype(jnp.int32) for name in ("h", "x", "c"))
    own = pl.multiple_of(((h * XS + x) * CS + c) * FW, FW)
    bias = jnp.concatenate([wide[pl.ds(own, FW), :]] * ROWS, axis=0)
    out_ref[...] = placed_sum(0, msg_ref, meta_ref) + bias


def dense_kernel(agg_ref, w1_ref, b1_ref, w2_ref, out_ref):
    half = HS * XC
    agg = [agg_ref[FEAT_PLACE[m]].astype(F32) + agg_ref[FEAT_PLACE[half + m]].astype(F32) for m in range(half)]
    agg = [jnp.concatenate([part[i * FW : (i + 1) * FW] for part in agg], axis=0) for i in range(2)]
    agg = jnp.concatenate(agg, axis=1)
    hidden = lax.dot_general(w1_ref[...], agg.astype(BF), TN, preferred_element_type=F32)
    bias = column(b1_ref)
    hidden = jnp.maximum(hidden + jnp.concatenate([bias, bias], axis=1), 0.0).astype(BF)
    own = pl.multiple_of(lax.axis_index("h").astype(jnp.int32) * (XC * FW), XC * FW)
    out = lax.dot_general(w2_ref[:, pl.ds(own, XC * FW)], hidden, TN, preferred_element_type=F32).astype(BF)
    for i in range(2):
        for e in range(XC):
            out_ref[PLANE_PLACE[e], i] = out[e * FW : (e + 1) * FW, i * BLK : (i + 1) * BLK]


def call(kernel, name, out_shape, *args, in_specs=None, scratch_shapes=()):
    return pl.pallas_call(
        kernel,
        in_specs=in_specs or [VMEM] * len(args),
        out_specs=jax.tree.map(lambda _: VMEM, out_shape),
        out_shape=out_shape,
        scratch_shapes=scratch_shapes,
        compiler_params=ROOM,
        name=name,
    )(*args)


def per_device(features, tiles, rows, cols, counts, w1, b1, w2, b2):
    cols, rows = (jnp.swapaxes(table, 1, 2) for table in (cols, rows))
    cols, rows, counts, features = (in_hbm(array) for array in (cols, rows, counts, features))
    b1, b2 = b1[None, :], b2[None, :]
    smem = [pltpu.SMEM(table.shape, table.dtype) for table in (cols, counts, rows)]
    copy_sems = pltpu.SemaphoreType.DMA

    def message(lines):
        return jax.ShapeDtypeStruct((ZQ * YS, lines, BLK), BF)

    def quad_exchange(msg):
        return lax.all_to_all(msg, ("b", "y"), 0, 0, axis_index_groups=[QUAD_ORDER], tiled=True)

    msg1, held, pick = call(
        first_terms_kernel,
        "first_terms",
        (message(BODY + META), pltpu.VMEM((STEPS, YS, CAP, BLK, BLK), BF), pltpu.VMEM((STEPS * YS * MSG, LINES), BF)),
        cols,
        counts,
        rows,
        features,
        in_hbm(tiles.reshape(1, STEPS, YS, CAP, BLK, BLK)),
        in_specs=[HBM] * 5,
        scratch_shapes=[*smem, pltpu.VMEM(features.shape, BF), copy_sems((4 + STEPS // WAVE,))],
    )
    msg1 = quad_exchange(msg1)
    sums = call(first_sum_kernel, "first_sum", jax.ShapeDtypeStruct((QUADS * HS * XC, 2 * FW, BLK), BF), msg1)
    sums = lax.all_to_all(sums, ("q", "h", "x", "c"), 0, 0, axis_index_groups=[FEAT_ORDER], tiled=True)
    z = call(dense_kernel, "dense", jax.ShapeDtypeStruct((XC, 2, FW, BLK), BF), sums, w1, b1, w2)
    z = lax.all_to_all(z, ("x", "c"), 0, 0, axis_index_groups=[PLANE_ORDER], tiled=True).reshape(ROWS, FW, BLK)

    msg2 = call(second_terms_kernel, "second_terms", message(BODY), pick, z, held)
    msg2 = quad_exchange(msg2)
    far = call(far_sum_kernel, "far_sum", jax.ShapeDtypeStruct((LINES, BLK), BF), msg2, msg1)
    far = lax.ppermute(far, "q", [(0, 1), (1, 0)])
    near = call(
        near_sum_kernel,
        "near_sum",
        jax.ShapeDtypeStruct((LINES, BLK), F32),
        msg2,
        msg1,
        b2,
        scratch_shapes=[pltpu.VMEM((b2.shape[1], BLK), F32)],
    )
    return (near + far.astype(F32)).reshape(ROWS, FW, BLK)


def solution(mesh):
    fine = Mesh(mesh.devices.reshape(QUADS, ZQ, YS, HS, XS, CS), ("q", "b", "y", "h", "x", "c"))
    dom, feat = ("q", "b", "y"), ("h", "x", "c")
    placed = (
        P(dom, feat, None),
        P(dom, None, None, None, None),
        P(dom, None, None),
        P(dom, None, None),
        P(dom, None),
        P(),
        P(),
        P(),
        P(),
    )
    return jax.shard_map(
        per_device, mesh=fine, in_specs=placed, out_specs=P(dom, feat, None), check_vma=False
    )
```

```python
import functools

import jax
import jax.numpy as jnp
from jax import lax
from jax.experimental import pallas as pl
from jax.experimental.pallas import tpu as pltpu
from jax.sharding import Mesh
from jax.sharding import PartitionSpec as P

QUADS, ZQ, YS, HS, XS, CS = 2, 4, 4, 2, 4, 2
XC = XS * CS
STEPS = QUADS * ZQ
WAVE = 2
CAP, BLK, FW, ROWS = 4, 128, 16, 16
MSG = CAP * FW
BODY = QUADS * MSG
META = 8
LINES = ROWS * FW
BF, F32 = jnp.bfloat16, jnp.float32


def led_by(first, size, hops):
    order = [first] + sorted((m for m in range(size) if m != first), key=lambda m: -hops(m, first))
    return order, [order.index(m) for m in range(size)]


def ring(a, b, size):
    return min((a - b) % size, (b - a) % size)


def quad_hops(m, n):
    return abs(m // YS - n // YS) + ring(m % YS, n % YS, YS)


def plane_hops(m, n):
    return ring(m // CS, n // CS, XS) + (m % CS != n % CS)


def feat_hops(m, n):
    z, w = ((k // XC % HS) * QUADS + k // XC // HS for k in (m, n))
    return ZQ * ring(z, w, QUADS * HS) + plane_hops(m % XC, n % XC)


QUAD_ORDER, QUAD_PLACE = led_by(1 * YS + 2, ZQ * YS, quad_hops)
FEAT_FIRST = (0 * HS + 1) * XC + 2 * CS + 1
FEAT_ORDER, FEAT_PLACE = led_by(FEAT_FIRST, QUADS * HS * XC, feat_hops)
PLANE_ORDER, PLANE_PLACE = led_by(2 * CS + 1, XC, plane_hops)
VMEM = pl.BlockSpec(memory_space=pltpu.VMEM)
HBM = pl.BlockSpec(memory_space=pltpu.HBM)
NT = (((1,), (1,)), ((), ()))
TN = (((0,), (0,)), ((), ()))
ROOM = pltpu.CompilerParams(vmem_limit_bytes=8 << 20)


def in_hbm(array):
    return pltpu.with_memory_space_constraint(array, pltpu.HBM)


def target(step, y):
    q = lax.axis_index("q").astype(jnp.int32)
    return ((step // ZQ ^ q) * ZQ + step % ZQ) * YS + y


def write_terms(step, cols_ref, counts_ref, values_ref, tiles_ref, out_ref):
    for y in range(YS):
        p = target(step, y)
        count = counts_ref[0, p]
        for j in range(0, CAP, 2):
            pair = jnp.concatenate([values_ref[cols_ref[0, j + i, p]] for i in range(2)], axis=0)
            tiles = tiles_ref[step, y, j : j + 2].reshape(2 * BLK, BLK)
            term = lax.dot_general(pair, tiles, NT, preferred_element_type=F32)
            for i in range(2):
                mine = term[i * FW : (i + 1) * FW, i * BLK : (i + 1) * BLK]
                mine = jnp.where(j + i < count, mine, 0.0).astype(BF)
                at = (step // ZQ) * MSG + (j + i) * FW
                out_ref[QUAD_PLACE[step % ZQ * YS + y], at : at + FW, :] = mine


def first_terms_kernel(
    cols_in, counts_in, rows_in, values_in, tiles_in, out_ref, tiles_ref, cols, counts, rows, values, sems
):
    small = list(zip((cols_in, counts_in, rows_in, values_in), (cols, counts, rows, values)))
    copies = [pltpu.make_async_copy(src, dst, sems.at[i]) for i, (src, dst) in enumerate(small)]
    for step in range(0, STEPS, WAVE):
        chunk = tiles_in.at[0, pl.ds(target(step, 0) // YS, WAVE)]
        copies.append(pltpu.make_async_copy(chunk, tiles_ref.at[pl.ds(step, WAVE)], sems.at[len(copies)]))
    for copy in copies:
        copy.start()
    for copy in copies[: len(small)]:
        copy.wait()
    lane = lax.broadcasted_iota(jnp.int32, (META, BLK), 1)
    for b in range(ZQ):
        for y in range(YS):
            place = lane % FW
            for r in range(QUADS):
                for j in range(CAP):
                    row = rows[0, j, target(r * ZQ + b, y)]
                    place = jnp.where(lane // FW == r * CAP + j, place + row * FW, place)
            out_ref[QUAD_PLACE[b * YS + y], BODY:, :] = place.astype(F32).astype(BF)
    for step in range(STEPS):
        if step % WAVE == 0:
            copies[len(small) + step // WAVE].wait()
        write_terms(step, cols, counts, values, tiles_ref, out_ref)


def second_terms_kernel(cols_in, counts_in, values_ref, tiles_ref, out_ref, cols, counts, sems):
    copies = [pltpu.make_async_copy(cols_in, cols, sems.at[0]), pltpu.make_async_copy(counts_in, counts, sems.at[1])]
    for copy in copies:
        copy.start()
    for copy in copies:
        copy.wait()
    for step in range(STEPS):
        write_terms(step, cols, counts, values_ref, tiles_ref, out_ref)


def placed_sum(r, msg_ref, meta_ref):
    total = jnp.zeros((LINES, BLK), F32)
    low = lax.broadcasted_iota(jnp.int32, (META, BLK), 1) < MSG
    spot = lax.broadcasted_iota(jnp.int32, (LINES, BLK), 0).astype(F32)
    for s in range(0, ZQ * YS, 4):
        halves = []
        for t in (s, s + 2):
            here, there = (meta_ref[t + i, BODY:, :].astype(F32) for i in range(2))
            if r == 0:
                there = pltpu.roll(there, MSG, 1)
            else:
                here = pltpu.roll(here, MSG, 1)
            place = jnp.concatenate([jnp.where(low, here, there)] * (LINES // META), axis=0)
            halves.append(jnp.where(spot == place, 1.0, 0.0).astype(BF))
        put = jnp.concatenate(halves, axis=1)
        lines = jnp.concatenate([msg_ref[s + i, r * MSG : (r + 1) * MSG, :] for i in range(4)], axis=0)
        total += jnp.dot(put, lines, preferred_element_type=F32)
    return total


def first_sum_kernel(msg_ref, out_ref):
    for r in range(QUADS):
        total = placed_sum(r, msg_ref, msg_ref).astype(BF)
        quad = r ^ lax.axis_index("q").astype(jnp.int32)
        for h in range(HS):
            for e in range(XC):
                member = h * XC + e
                place = jnp.where(quad == 0, FEAT_PLACE[member], FEAT_PLACE[HS * XC + member])
                rows = PLANE_PLACE[e] * 2 * FW
                out_ref[place] = total[rows : rows + 2 * FW]


def far_sum_kernel(msg_ref, meta_ref, out_ref):
    out_ref[...] = placed_sum(1, msg_ref, meta_ref).astype(BF)


def column(bias_ref):
    return jnp.transpose(jnp.broadcast_to(bias_ref[...], (BLK, bias_ref.shape[1])))


def near_sum_kernel(msg_ref, meta_ref, bias_ref, out_ref, wide):
    wide[...] = column(bias_ref)
    h, x, c = (lax.axis_index(name).astype(jnp.int32) for name in ("h", "x", "c"))
    own = pl.multiple_of(((h * XS + x) * CS + c) * FW, FW)
    bias = jnp.concatenate([wide[pl.ds(own, FW), :]] * ROWS, axis=0)
    out_ref[...] = placed_sum(0, msg_ref, meta_ref) + bias


def dense_kernel(agg_ref, w1_ref, b1_ref, w2_ref, out_ref):
    half = HS * XC
    agg = [agg_ref[FEAT_PLACE[m]].astype(F32) + agg_ref[FEAT_PLACE[half + m]].astype(F32) for m in range(half)]
    agg = [jnp.concatenate([part[i * FW : (i + 1) * FW] for part in agg], axis=0) for i in range(2)]
    agg = jnp.concatenate(agg, axis=1)
    hidden = lax.dot_general(w1_ref[...], agg.astype(BF), TN, preferred_element_type=F32)
    bias = column(b1_ref)
    hidden = jnp.maximum(hidden + jnp.concatenate([bias, bias], axis=1), 0.0).astype(BF)
    own = pl.multiple_of(lax.axis_index("h").astype(jnp.int32) * (XC * FW), XC * FW)
    out = lax.dot_general(w2_ref[:, pl.ds(own, XC * FW)], hidden, TN, preferred_element_type=F32).astype(BF)
    for i in range(2):
        for e in range(XC):
            out_ref[PLANE_PLACE[e], i] = out[e * FW : (e + 1) * FW, i * BLK : (i + 1) * BLK]


def call(kernel, name, out_shape, *args, in_specs=None, scratch_shapes=()):
    return pl.pallas_call(
        kernel,
        in_specs=in_specs or [VMEM] * len(args),
        out_specs=jax.tree.map(lambda _: VMEM, out_shape),
        out_shape=out_shape,
        scratch_shapes=scratch_shapes,
        compiler_params=ROOM,
        name=name,
    )(*args)


def per_device(features, tiles, rows, cols, counts, w1, b1, w2, b2):
    cols, rows = (jnp.swapaxes(table, 1, 2) for table in (cols, rows))
    cols, rows, counts, features = (in_hbm(array) for array in (cols, rows, counts, features))
    b1, b2 = b1[None, :], b2[None, :]
    smem = [pltpu.SMEM(table.shape, table.dtype) for table in (cols, counts, rows)]
    copy_sems = pltpu.SemaphoreType.DMA

    def message(lines):
        return jax.ShapeDtypeStruct((ZQ * YS, lines, BLK), BF)

    def quad_exchange(msg):
        return lax.all_to_all(msg, ("b", "y"), 0, 0, axis_index_groups=[QUAD_ORDER], tiled=True)

    msg1, held = call(
        first_terms_kernel,
        "first_terms",
        (message(BODY + META), pltpu.VMEM((STEPS, YS, CAP, BLK, BLK), BF)),
        cols,
        counts,
        rows,
        features,
        in_hbm(tiles.reshape(1, STEPS, YS, CAP, BLK, BLK)),
        in_specs=[HBM] * 5,
        scratch_shapes=[*smem, pltpu.VMEM(features.shape, BF), copy_sems((4 + STEPS // WAVE,))],
    )
    msg1 = quad_exchange(msg1)
    sums = call(first_sum_kernel, "first_sum", jax.ShapeDtypeStruct((QUADS * HS * XC, 2 * FW, BLK), BF), msg1)
    sums = lax.all_to_all(sums, ("q", "h", "x", "c"), 0, 0, axis_index_groups=[FEAT_ORDER], tiled=True)
    z = call(dense_kernel, "dense", jax.ShapeDtypeStruct((XC, 2, FW, BLK), BF), sums, w1, b1, w2)
    z = lax.all_to_all(z, ("x", "c"), 0, 0, axis_index_groups=[PLANE_ORDER], tiled=True).reshape(ROWS, FW, BLK)

    msg2 = call(
        second_terms_kernel,
        "second_terms",
        message(BODY),
        cols,
        counts,
        z,
        held,
        in_specs=[HBM, HBM, VMEM, VMEM],
        scratch_shapes=[*smem[:2], copy_sems((2,))],
    )
    msg2 = quad_exchange(msg2)
    far = call(far_sum_kernel, "far_sum", jax.ShapeDtypeStruct((LINES, BLK), BF), msg2, msg1)
    far = lax.ppermute(far, "q", [(0, 1), (1, 0)])
    near = call(
        near_sum_kernel,
        "near_sum",
        jax.ShapeDtypeStruct((LINES, BLK), F32),
        msg2,
        msg1,
        b2,
        scratch_shapes=[pltpu.VMEM((b2.shape[1], BLK), F32)],
    )
    return (near + far.astype(F32)).reshape(ROWS, FW, BLK)


def solution(mesh):
    fine = Mesh(mesh.devices.reshape(QUADS, ZQ, YS, HS, XS, CS), ("q", "b", "y", "h", "x", "c"))
    dom, feat = ("q", "b", "y"), ("h", "x", "c")
    placed = (
        P(dom, feat, None),
        P(dom, None, None, None, None),
        P(dom, None, None),
        P(dom, None, None),
        P(dom, None),
        P(),
        P(),
        P(),
        P(),
    )
    return jax.shard_map(
        per_device, mesh=fine, in_specs=placed, out_specs=P(dom, feat, None), check_vma=False
    )
```
